32 devices in a mesh: gx: 4 (over z), gy: 8 (over y, x, core).
Axes of the slice: x: 2, y: 2, z: 4, core: 2. Of those that a mesh axis runs over, the one named last changes fastest.
Arguments:
- leaf_maps: float32 [4, 8, 512, 512], P('gx', 'gy'), may hold values from -8 to 20, as said below
- leaf_fluxes: float32 [4, 8, 512, 128], P('gx', 'gy'), may hold values from -24 to 24
Outputs:
- boundary_values: float32 [4, 8, 512, 128], P('gx', 'gy')
The draws below stay inside these ranges and needn't reach their ends.
Inputs may be any that keep to these rules, and one draw needn't show every extreme that they name: `leaf_maps`: every leaf's map is symmetric and positive definite with smallest eigenvalue 0.1 or more.
All inputs are finite; a program needn't handle non-finite values.
Results may differ from the reference program's by a relative error of at most 0.0003.
Values sent between devices are 32-bit elements; how exact they have to be, the bound alone decides.
A program may use at most 128 MiB of HBM per device.

```python
import math
from functools import partial
import jax
import jax.numpy as jnp
from jax import lax

PATCH = 128
SOURCES = 128
LEVELS = 4
PCOLS = 4
PROWS = 8


def draw_leaf_maps(key, part):
    points = 4 * PATCH
    first_key, second_key, third_key = jax.random.split(key, 3)
    shape_all = (PCOLS, PROWS, points, points)
    mixing = jax.random.normal(first_key, shape_all, jnp.float32)
    diagonal_part = jnp.exp(jax.random.uniform(second_key, (PCOLS, PROWS, points), jnp.float32, math.log(0.3), math.log(1.0)))
    bond_weights = jax.random.uniform(third_key, (PCOLS, PROWS, points), jnp.float32, 1.0, 4.0)
    mixed_part = jnp.einsum('abij,abkj->abik', mixing, mixing) / points
    point_index = jnp.arange(points)
    inside_edge = (point_index % PATCH != PATCH - 1).astype(jnp.float32)
    bond_weights = bond_weights * inside_edge
    previous = jnp.concatenate([jnp.zeros_like(bond_weights[..., :1]), bond_weights[..., :-1]], axis=-1)
    upper_shift = (point_index[:, None] + 1 == point_index[None, :]).astype(jnp.float32)
    coupling = bond_weights[..., :, None] * upper_shift
    laplace = -coupling - jnp.swapaxes(coupling, -1, -2)
    eye_matrix = jnp.eye(points, dtype=jnp.float32)
    return mixed_part + laplace + (diagonal_part + bond_weights + previous)[..., :, None] * eye_matrix


def shard_levels(key, shape, cuts, low, top_value):
    def one(dim, blocks):
        heights = jax.random.uniform(jax.random.fold_in(jax.random.fold_in(key, 6), dim), (blocks,), jnp.float32, low / len(cuts), top_value / len(cuts))
        return jnp.repeat(jnp.exp(heights), shape[dim] // blocks).reshape((-1,) + (1,) * (len(shape) - dim - 1))

    factor_of = one(*cuts[0])
    for cut in cuts[1:]:
        factor_of = factor_of * one(*cut)
    return factor_of


def noise(key, extent, spread, limit, cuts=(), kind=jnp.bfloat16):
    entries = spread * jax.random.normal(key, extent, jnp.float32)
    if cuts:
        entries = entries * shard_levels(key, extent, cuts, -0.22, 0.18)
    return jnp.clip(entries, -limit, limit).astype(kind)


def setup_inputs(seed: int = 0) -> dict:
    arg_keys = jax.random.split(jax.random.key(seed), 3)
    return {
        "leaf_maps": draw_leaf_maps(jax.random.fold_in(arg_keys[2], 71), 0),
        "leaf_fluxes": noise(arg_keys[1], (PCOLS, PROWS, 4 * PATCH, SOURCES), 4.0, 24.0, ((0, 4), (1, 8)), jnp.float32),
    }


side_names = ('left', 'right', 'bottom', 'top')

def side_spans(cols_count, rows_count, patch_side):
    lengths = {'left': rows_count * patch_side, 'right': rows_count * patch_side, 'bottom': cols_count * patch_side, 'top': cols_count * patch_side}
    starts = {}
    running = 0
    for side_name in side_names:
        starts[side_name] = running
        running = running + lengths[side_name]
    return (starts, lengths)

def merge_layout(direction):
    if direction == 'y':
        return (('top', 'bottom'), ((0, 'left'), (1, 'left'), (0, 'right'), (1, 'right'), (0, 'bottom'), (1, 'top')))
    return (('right', 'left'), ((0, 'left'), (1, 'right'), (0, 'bottom'), (1, 'bottom'), (0, 'top'), (1, 'top')))

def level_plan(levels):
    merge_plan = []
    cols_count, rows_count = (1, 1)
    for tree_level in range(levels):
        if tree_level % 2 == 0:
            merge_plan.append(('y', cols_count, rows_count))
            rows_count = rows_count * 2
        else:
            merge_plan.append(('x', cols_count, rows_count))
            cols_count = cols_count * 2
    return merge_plan

def take_rows(matrix, starts, lengths, side_name):
    return matrix[starts[side_name]:starts[side_name] + lengths[side_name]]

def take_block(matrix, starts, lengths, row_side, col_side):
    rows_part = take_rows(matrix, starts, lengths, row_side)
    return rows_part[:, starts[col_side]:starts[col_side] + lengths[col_side]]

def product(left_part, right_part):
    return jnp.dot(left_part, right_part, precision=lax.Precision.HIGHEST)

def solve_with(factor, rhs_part):
    halfway = jax.scipy.linalg.solve_triangular(factor, rhs_part, lower=True)
    return jax.scipy.linalg.solve_triangular(factor, halfway, lower=True, trans=1)

def diagonal_rows(matrix, starts, lengths, child_index, row_side, pieces):
    blocks = []
    for other_index, col_side in pieces:
        if other_index == child_index:
            blocks.append(take_block(matrix, starts, lengths, row_side, col_side))
        else:
            blocks.append(jnp.zeros((lengths[row_side], lengths[col_side]), matrix.dtype))
    return jnp.concatenate(blocks, axis=1)

def merge_pair(maps_pair, fluxes_pair, direction, cols_count, rows_count, patch_side):
    starts, lengths = side_spans(cols_count, rows_count, patch_side)
    face_sides, pieces = merge_layout(direction)
    interface_matrix = take_block(maps_pair[0], starts, lengths, face_sides[0], face_sides[0]) + take_block(maps_pair[1], starts, lengths, face_sides[1], face_sides[1])
    factor = jnp.linalg.cholesky(interface_matrix)
    across = jnp.concatenate([take_block(maps_pair[child_index], starts, lengths, face_sides[child_index], side_name) for child_index, side_name in pieces], axis=1)
    inward = jnp.concatenate([take_block(maps_pair[child_index], starts, lengths, side_name, face_sides[child_index]) for child_index, side_name in pieces], axis=0)
    face_flux = take_rows(fluxes_pair[0], starts, lengths, face_sides[0]) + take_rows(fluxes_pair[1], starts, lengths, face_sides[1])
    solved = solve_with(factor, across)
    weights = solve_with(factor, face_flux)
    assembled = jnp.concatenate([diagonal_rows(maps_pair[child_index], starts, lengths, child_index, side_name, pieces) for child_index, side_name in pieces], axis=0)
    merged_map = assembled - product(inward, solved)
    outer_flux = jnp.concatenate([take_rows(fluxes_pair[child_index], starts, lengths, side_name) for child_index, side_name in pieces], axis=0)
    merged_flux = outer_flux - product(inward, weights)
    return (merged_map, merged_flux, solved, weights)

def merge_vector(lower_map, upper_map, lower_flux, upper_flux, direction, cols_count, rows_count, patch_side):
    return merge_pair((lower_map, upper_map), (lower_flux, upper_flux), direction, cols_count, rows_count, patch_side)

def top_vector(lower_map, upper_map, lower_flux, upper_flux, direction, cols_count, rows_count, patch_side):
    starts, lengths = side_spans(cols_count, rows_count, patch_side)
    face_sides, pieces = merge_layout(direction)
    interface_matrix = take_block(lower_map, starts, lengths, face_sides[0], face_sides[0]) + take_block(upper_map, starts, lengths, face_sides[1], face_sides[1])
    factor = jnp.linalg.cholesky(interface_matrix)
    face_flux = take_rows(lower_flux, starts, lengths, face_sides[0]) + take_rows(upper_flux, starts, lengths, face_sides[1])
    return solve_with(factor, face_flux)

def merged_length(direction, cols_count, rows_count, patch_side):
    starts, lengths = side_spans(cols_count, rows_count, patch_side)
    face_sides, pieces = merge_layout(direction)
    return sum((lengths[side_name] for child_index, side_name in pieces))

def child_values(group_values, face_values, direction, cols_count, rows_count, patch_side, child_index):
    starts, lengths = side_spans(cols_count, rows_count, patch_side)
    face_sides, pieces = merge_layout(direction)
    offsets = {}
    running = 0
    for each_piece in pieces:
        offsets[each_piece] = running
        running = running + lengths[each_piece[1]]
    parts_list = []
    for side_name in side_names:
        if side_name == face_sides[child_index]:
            parts_list.append(face_values)
        else:
            first_row = offsets[child_index, side_name]
            parts_list.append(group_values[first_row:first_row + lengths[side_name]])
    return jnp.concatenate(parts_list, axis=0)

def pair_split(stacked_array, direction):
    if direction == 'y':
        return (stacked_array[:, 0::2], stacked_array[:, 1::2])
    return (stacked_array[0::2], stacked_array[1::2])

def pair_join(lower_part, upper_part, direction):
    if direction == 'y':
        joined = jnp.stack([lower_part, upper_part], axis=2)
        return joined.reshape((joined.shape[0], joined.shape[1] * 2) + joined.shape[3:])
    joined = jnp.stack([lower_part, upper_part], axis=1)
    return joined.reshape((joined.shape[0] * 2,) + joined.shape[2:])

def over_groups(function):
    return jax.vmap(jax.vmap(function))

def reference(leaf_maps, leaf_fluxes):
    patch_side = leaf_maps.shape[2] // 4
    merge_plan = level_plan(LEVELS)
    level_maps, fluxes = (leaf_maps, leaf_fluxes)
    stored = []
    top_weights = None
    for tree_level in range(LEVELS):
        direction, cols_count, rows_count = merge_plan[tree_level]
        lower_maps, upper_maps = pair_split(level_maps, direction)
        lower_fluxes, upper_fluxes = pair_split(fluxes, direction)
        if tree_level < LEVELS - 1:
            merger = partial(merge_vector, direction=direction, cols_count=cols_count, rows_count=rows_count, patch_side=patch_side)
            level_maps, fluxes, solved, weights = over_groups(merger)(lower_maps, upper_maps, lower_fluxes, upper_fluxes)
            stored.append((solved, weights))
        else:
            top_solver = partial(top_vector, direction=direction, cols_count=cols_count, rows_count=rows_count, patch_side=patch_side)
            top_weights = over_groups(top_solver)(lower_maps, upper_maps, lower_fluxes, upper_fluxes)
    direction, cols_count, rows_count = merge_plan[LEVELS - 1]
    face_values = -top_weights
    group_length = merged_length(direction, cols_count, rows_count, patch_side)
    group_values = jnp.zeros(face_values.shape[:2] + (group_length, face_values.shape[3]), face_values.dtype)
    for tree_level in range(LEVELS - 1, -1, -1):
        direction, cols_count, rows_count = merge_plan[tree_level]
        if tree_level < LEVELS - 1:
            solved, weights = stored[tree_level]
            face_values = -(over_groups(product)(solved, group_values) + weights)
        lower_values = over_groups(partial(child_values, direction=direction, cols_count=cols_count, rows_count=rows_count, patch_side=patch_side, child_index=0))(group_values, face_values)
        upper_values = over_groups(partial(child_values, direction=direction, cols_count=cols_count, rows_count=rows_count, patch_side=patch_side, child_index=1))(group_values, face_values)
        group_values = pair_join(lower_values, upper_values, direction)
    return group_values
```

```python
import jax
import jax.numpy as jnp
from jax import lax
from jax.experimental import pallas as pl
from jax.experimental.pallas import tpu as pltpu
from jax.sharding import PartitionSpec as P

F32 = jnp.float32
HIGHEST = lax.Precision.HIGHEST
ROWS_DIM = (((0,), (0,)), ((), ()))
PANEL = 16


def dot(left, right):
    return jnp.dot(left, right, precision=HIGHEST, preferred_element_type=F32)


def tdot(left, right):
    return lax.dot_general(
        left, right, ROWS_DIM, precision=HIGHEST, preferred_element_type=F32
    )


def three_parts(x):
    first = x.astype(jnp.bfloat16)
    rest = x - first.astype(F32)
    second = rest.astype(jnp.bfloat16)
    third = (rest - second.astype(F32)).astype(jnp.bfloat16)
    return first, second, third


def tdot_thin(left, right):
    a, b, c = three_parts(left)
    d, e, f = three_parts(right)
    return lax.dot_general(
        jnp.concatenate([a, a, b, b, a, c], axis=0),
        jnp.concatenate([d, e, d, e, f, d], axis=0),
        ROWS_DIM,
        preferred_element_type=F32,
    )


def panel_solve(rows, rhs, first):
    width, lanes = rows.shape
    sub = lax.broadcasted_iota(jnp.int32, (width, lanes), 0)
    cols = [
        jnp.broadcast_to(rows[:, first + j : first + j + 1], (width, lanes))
        for j in range(width)
    ]
    for j in range(0, width, 2):
        c0, c1 = cols[j], cols[j + 1]
        aa, bb, dd = c0[j : j + 1], c1[j : j + 1], c1[j + 1 : j + 2]
        scale = 1.0 / (aa * dd - bb * bb)
        aa, bb, dd = aa * scale, bb * scale, dd * scale

        def step(x):
            x0, x1 = x[j : j + 1], x[j + 1 : j + 2]
            r0 = dd * x0 - bb * x1
            r1 = aa * x1 - bb * x0
            y = x - c0 * r0 - c1 * r1
            return jnp.where(sub == j, r0, jnp.where(sub == j + 1, r1, y))

        rhs = step(rhs)
        for m in range(j + 2, width):
            cols[m] = step(cols[m])
    return rhs


def spd_inverse(a):
    size = a.shape[0]
    row = lax.broadcasted_iota(jnp.int32, (PANEL, size), 0)
    col = lax.broadcasted_iota(jnp.int32, (PANEL, size), 1)
    for first in range(0, size, PANEL):
        rows = a[first : first + PANEL]
        v = rows - jnp.where(col == row + first, 1.0, 0.0)
        a = a - tdot_thin(v, panel_solve(rows, v, first))
    row = lax.broadcasted_iota(jnp.int32, (size, size), 0)
    col = lax.broadcasted_iota(jnp.int32, (size, size), 1)
    return jnp.where(row == col, 2.0, 0.0) - a


def block_solve(g, face, p, schur=None):
    for k in range(0, face, p):
        head = g[k : k + p, k + p :]
        t = dot(spd_inverse(g[k : k + p, k : k + p]), head)
        if k + p < face:
            g[k + p : face, k + p :] -= tdot(head[:, : face - k - p], t)
        if schur is not None:
            outer = head[:, face - k - p : face - k - p + schur.shape[0]]
            schur[...] -= tdot(outer, t[:, face - k - p :])
        g[k : k + p, k + p :] = t
    for k in range(face - 2 * p, -1, -p):
        g[k : k + p, face:] -= dot(g[k : k + p, k + p : face], g[k + p : face, face:])


def leaf_merge(own_map, own_flux, other_map, other_flux, n_ref, y_ref, send_ref, g):
    p = own_map.shape[0] // 4
    gx, gy = lax.axis_index("gx"), lax.axis_index("gy")
    lower = gy % 2 == 0
    low_group = (gy // 2) % 2 == 0
    f1 = pl.multiple_of(p * (1 - gx % 2), p)
    out = pl.multiple_of(p * (gx % 2), p)
    bottom, top = 2 * p, 3 * p

    def lo(r, c):
        at = (pl.ds(r, p), pl.ds(c, p))
        return jnp.where(lower, own_map[at], other_map[at])

    def up(r, c):
        at = (pl.ds(r, p), pl.ds(c, p))
        return jnp.where(lower, other_map[at], own_map[at])

    def lo_h(r):
        return jnp.where(lower, own_flux[pl.ds(r, p), :], other_flux[pl.ds(r, p), :])

    def up_h(r):
        return jnp.where(lower, other_flux[pl.ds(r, p), :], own_flux[pl.ds(r, p), :])

    g[:, 0:p] = lo(top, top) + up(bottom, bottom)
    g[:, p : 2 * p] = lo(top, f1)
    g[:, 2 * p : 3 * p] = up(bottom, f1)
    g[:, 3 * p : 4 * p] = jnp.where(low_group, up(bottom, top), lo(top, bottom))
    g[:, 4 * p : 5 * p] = lo(top, out)
    g[:, 5 * p : 6 * p] = up(bottom, out)
    g[:, 6 * p :] = lo_h(top) + up_h(bottom)
    none = jnp.zeros((p, p), F32)
    from_lo = jnp.where(low_group, 0.0, 1.0)
    from_up = 1.0 - from_lo
    blocks = [
        [lo(f1, f1), none, lo(f1, bottom) * from_lo, lo(f1, out), none, lo_h(f1)],
        [none, up(f1, f1), up(f1, top) * from_up, none, up(f1, out), up_h(f1)],
        [
            lo(bottom, f1) * from_lo,
            up(top, f1) * from_up,
            jnp.where(low_group, up(top, top), lo(bottom, bottom)),
            lo(bottom, out) * from_lo,
            up(top, out) * from_up,
            jnp.where(low_group, up_h(top), lo_h(bottom)),
        ],
        [lo(out, f1), none, lo(out, bottom) * from_lo, lo(out, out), none, lo_h(out)],
        [none, up(out, f1), up(out, top) * from_up, none, up(out, out), up_h(out)],
    ]
    for i, line in enumerate(blocks):
        for j, block in enumerate(line):
            n_ref[i * p : (i + 1) * p, j * p : j * p + block.shape[1]] = block
    block_solve(g, p, p, n_ref)
    y_ref[...] = g[:, p:]
    half = 3 * p // 2
    mine = pl.ds(pl.multiple_of((gy % 2) * half, half), half)
    send_ref[:, : 3 * p] = n_ref[mine, : 3 * p]
    send_ref[:, 3 * p :] = n_ref[mine, 5 * p :]


def column_merge(n0, got, swapped, n_ref, y_ref, send2_ref, send3_ref, g, q):
    p = n0.shape[0] // 5
    core = lax.axis_index("gy") % 2
    half = 3 * p // 2
    q[pl.ds(pl.multiple_of(core * half, half), half), :] = got[...]
    q[pl.ds(pl.multiple_of((1 - core) * half, half), half), :] = swapped[...]
    f, o, e = 2 * p, 3 * p, 5 * p
    g[:, 0:f] = n0[0:f, 0:f] + q[0:f, 0:f]
    g[:, f : f + p] = n0[0:f, f:o]
    g[:, f + p : f + 2 * p] = q[0:f, f:o]
    g[:, f + 2 * p : f + 4 * p] = n0[0:f, o:e]
    g[:, f + 4 * p :] = n0[0:f, e:] + q[0:f, o:]
    n_ref[...] = jnp.zeros_like(n_ref)
    n_ref[0:p, 0:p] = n0[f:o, f:o]
    n_ref[0:p, 2 * p :] = n0[f:o, o:]
    n_ref[p : 2 * p, p : 2 * p] = q[f:o, f:o]
    n_ref[p : 2 * p, 4 * p :] = q[f:o, o:]
    n_ref[2 * p :, 0:p] = n0[o:, f:o]
    n_ref[2 * p :, 2 * p :] = n0[o:, o:]
    block_solve(g, f, p, n_ref)
    y_ref[...] = g[:, f:]
    send2_ref[...] = n_ref[pl.ds(pl.multiple_of(core * p, p), p), :]
    send3_ref[...] = n_ref[pl.ds(pl.multiple_of((2 + core) * p, p), p), 2 * p :]


def row_merge(n1, got2, got3, swap2, swap3, n_ref, y_ref, send_ref, g, q2, q3):
    p = n1.shape[0] // 4
    core = lax.axis_index("gy") % 2
    here = pl.ds(pl.multiple_of(core * p, p), p)
    there = pl.ds(pl.multiple_of((1 - core) * p, p), p)
    q2[here, :] = got2[...]
    q2[there, :] = swap2[...]
    q3[here, :] = got3[...]
    q3[there, :] = swap3[...]
    f = 2 * p
    g[:, 0:f] = n1[0:f, 0:f] + q2[:, 0:f]
    g[:, f : 2 * f] = n1[0:f, f : 2 * f]
    g[:, 2 * f : 3 * f] = q2[:, f : 2 * f]
    g[:, 3 * f :] = n1[0:f, 2 * f :] + q2[:, 2 * f :]
    n_ref[...] = jnp.zeros_like(n_ref)
    n_ref[0:f, 0:f] = n1[f:, f : 2 * f]
    n_ref[0:f, 2 * f :] = n1[f:, 2 * f :]
    n_ref[f:, f:] = q3[...]
    block_solve(g, f, p, n_ref)
    y_ref[...] = g[:, f:]
    send_ref[...] = n_ref[pl.ds(pl.multiple_of(core * f, f), f), :]


def top_solve(n2, got, swapped, y2, y1, u_ref, send_ref, g):
    p = n2.shape[0] // 4
    core = lax.axis_index("gy") % 2
    f = 2 * p
    here = pl.ds(pl.multiple_of(core * f, f), f)
    there = pl.ds(pl.multiple_of((1 - core) * f, f), f)
    g[here, :] = n2[here, :] + got[...]
    g[there, :] = n2[there, :] + swapped[...]
    block_solve(g, 4 * p, p)
    u3 = -g[:, 4 * p :]
    u2 = -(dot(y2[:, : 4 * p], u3) + y2[:, 4 * p :])
    u_ref[3 * p :, :] = u3[0:f]
    group = jnp.concatenate([u2, u3[0:f]], axis=0)
    u1 = -(dot(y1[:, : 4 * p], group) + y1[:, 4 * p :])
    u_ref[0:f, :] = u1
    u_ref[f : 3 * p, :] = u2[0:p]
    send_ref[0:f, :] = u1
    send_ref[f:, :] = u2[p:]


def leaf_values(own, got, y0, out_ref, u):
    p = own.shape[0] // 5
    gx, gy = lax.axis_index("gx"), lax.axis_index("gy")
    inner = (gx + 1) // 2 % 2 == 1
    lower = gy % 2 == 0
    low_group = (gy // 2) % 2 == 0
    u[0 : 3 * p, :] = jnp.where(inner, own[0 : 3 * p, :], got[...])
    u[3 * p :, :] = jnp.where(inner, own[3 * p :, :], 0.0)
    face = -(dot(y0[:, : 5 * p], u[...]) + y0[:, 5 * p :])
    spot = gy % 2
    near = u[pl.ds(pl.multiple_of(spot * p, p), p), :]
    far = u[pl.ds(pl.multiple_of((3 + spot) * p, p), p), :]
    cross = u[2 * p : 3 * p, :]
    f1_left = gx % 2 == 1
    out_ref[0:p, :] = jnp.where(f1_left, near, far)
    out_ref[p : 2 * p, :] = jnp.where(f1_left, far, near)
    out_ref[2 * p : 3 * p, :] = jnp.where(lower, jnp.where(low_group, 0.0, cross), face)
    out_ref[3 * p :, :] = jnp.where(lower, face, jnp.where(low_group, cross, 0.0))


def local(kernel, name, outs, scratch, *args):
    specs = [pl.BlockSpec(memory_space=pltpu.VMEM)]
    return pl.pallas_call(
        kernel,
        name=name,
        out_shape=[jax.ShapeDtypeStruct(shape, F32) for shape in outs],
        in_specs=specs * len(args),
        out_specs=specs * len(outs),
        scratch_shapes=[pltpu.VMEM(shape, F32) for shape in scratch],
        compiler_params=pltpu.CompilerParams(vmem_limit_bytes=48 << 20),
    )(*args)


def shards(leaf_maps, leaf_fluxes):
    p = leaf_maps.shape[2] // 4
    s = leaf_fluxes.shape[3]
    own_map, own_flux = leaf_maps[0, 0], leaf_fluxes[0, 0]
    columns, rows = lax.axis_size("gx"), lax.axis_size("gy")
    cores = [(i, i ^ 1) for i in range(rows)]
    groups = [(i, i ^ 2) for i in range(rows)]
    inner = [i for i in range(columns) if (i + 1) // 2 % 2 == 1]
    inward = [(i ^ 1, i) for i in inner]
    across = [(i, i ^ 3) for i in inner]
    outward = [(i, i ^ 1) for i in inner]

    def swap(x):
        return lax.ppermute(x, "gy", cores)

    other_map, other_flux = swap((own_map, own_flux))
    n0, y0, send = local(
        leaf_merge,
        "leaf_merge",
        [(5 * p, 5 * p + s), (p, 5 * p + s), (3 * p // 2, 3 * p + s)],
        [(p, 6 * p + s)],
        own_map,
        own_flux,
        other_map,
        other_flux,
    )
    got = lax.ppermute(send, "gx", inward)
    n1, y1, send2, send3 = local(
        column_merge,
        "column_merge",
        [(4 * p, 4 * p + s), (2 * p, 4 * p + s), (p, 4 * p + s), (p, 2 * p + s)],
        [(2 * p, 6 * p + s), (3 * p, 3 * p + s)],
        n0,
        got,
        swap(got),
    )
    got2, got3 = lax.ppermute((send2, send3), "gy", groups)
    swap2, swap3 = swap((got2, got3))
    n2, y2, send = local(
        row_merge,
        "row_merge",
        [(4 * p, 4 * p + s), (2 * p, 4 * p + s), (2 * p, 4 * p + s)],
        [(2 * p, 6 * p + s), (2 * p, 4 * p + s), (2 * p, 2 * p + s)],
        n1,
        got2,
        got3,
        swap2,
        swap3,
    )
    got = lax.ppermute(send, "gx", across)
    u, send = local(
        top_solve,
        "top_solve",
        [(5 * p, s), (3 * p, s)],
        [(4 * p, 4 * p + s)],
        n2,
        got,
        swap(got),
        y2,
        y1,
    )
    got = lax.ppermute(send, "gx", outward)
    (values,) = local(leaf_values, "leaf_values", [(4 * p, s)], [(5 * p, s)], u, got, y0)
    return values[None, None]


def solution(mesh):
    spec = P("gx", "gy", None, None)
    return jax.shard_map(
        shards, mesh=mesh, in_specs=(spec, spec), out_specs=spec, check_vma=False
    )
```

```python
import jax
import jax.numpy as jnp
from jax import lax
from jax.experimental import pallas as pl
from jax.experimental.pallas import tpu as pltpu
from jax.sharding import PartitionSpec as P

F32 = jnp.float32
HIGHEST = lax.Precision.HIGHEST
ROWS_DIM = (((0,), (0,)), ((), ()))
PANEL = 16


def dot(left, right):
    return jnp.dot(left, right, precision=HIGHEST, preferred_element_type=F32)


def tdot(left, right):
    return lax.dot_general(
        left, right, ROWS_DIM, precision=HIGHEST, preferred_element_type=F32
    )


def three_parts(x):
    first = x.astype(jnp.bfloat16)
    rest = x - first.astype(F32)
    second = rest.astype(jnp.bfloat16)
    third = (rest - second.astype(F32)).astype(jnp.bfloat16)
    return first, second, third


def tdot_thin(left, right):
    a, b, c = three_parts(left)
    d, e, f = three_parts(right)
    return lax.dot_general(
        jnp.concatenate([a, a, b, b, a, c], axis=0),
        jnp.concatenate([d, e, d, e, f, d], axis=0),
        ROWS_DIM,
        preferred_element_type=F32,
    )


def panel_solve(rows, rhs, first):
    width, lanes = rows.shape
    sub = lax.broadcasted_iota(jnp.int32, (width, lanes), 0)
    cols = [
        jnp.broadcast_to(rows[:, first + j : first + j + 1], (width, lanes))
        for j in range(width)
    ]
    for j in range(0, width, 2):
        c0, c1 = cols[j], cols[j + 1]
        aa, bb, dd = c0[j : j + 1], c1[j : j + 1], c1[j + 1 : j + 2]
        scale = 1.0 / (aa * dd - bb * bb)
        aa, bb, dd = aa * scale, bb * scale, dd * scale

        def step(x):
            x0, x1 = x[j : j + 1], x[j + 1 : j + 2]
            r0 = dd * x0 - bb * x1
            r1 = aa * x1 - bb * x0
            y = x - c0 * r0 - c1 * r1
            return jnp.where(sub == j, r0, jnp.where(sub == j + 1, r1, y))

        rhs = step(rhs)
        for m in range(j + 2, width):
            cols[m] = step(cols[m])
    return rhs


def spd_inverse(a):
    size = a.shape[0]
    row = lax.broadcasted_iota(jnp.int32, (PANEL, size), 0)
    col = lax.broadcasted_iota(jnp.int32, (PANEL, size), 1)
    for first in range(0, size, PANEL):
        rows = a[first : first + PANEL]
        v = rows - jnp.where(col == row + first, 1.0, 0.0)
        a = a - tdot_thin(v, panel_solve(rows, v, first))
    row = lax.broadcasted_iota(jnp.int32, (size, size), 0)
    col = lax.broadcasted_iota(jnp.int32, (size, size), 1)
    return jnp.where(row == col, 2.0, 0.0) - a


def block_solve(g, face, p, schur=None):
    for k in range(0, face, p):
        head = g[k : k + p, k + p :]
        t = dot(spd_inverse(g[k : k + p, k : k + p]), head)
        if k + p < face:
            g[k + p : face, k + p :] -= tdot(head[:, : face - k - p], t)
        if schur is not None:
            outer = head[:, face - k - p : face - k - p + schur.shape[0]]
            schur[...] -= tdot(outer, t[:, face - k - p :])
        g[k : k + p, k + p :] = t
    for k in range(face - 2 * p, -1, -p):
        g[k : k + p, face:] -= dot(g[k : k + p, k + p : face], g[k + p : face, face:])


def payload_blocks(count, p, s):
    spots = [(r * p, c * p, p) for r in range(count) for c in range(r, count)]
    return spots + [(r * p, -s, s) for r in range(count)]


def pack(send_ref, n_ref, count, p):
    half = p // 2
    core = lax.axis_index("gy") % 2
    width = n_ref.shape[1]
    at = 0
    for row, col, size in payload_blocks(count, p, width - n_ref.shape[0]):
        col = col % width
        rows = pl.ds(pl.multiple_of(row + core * half, half), half)
        send_ref[:, at : at + size] = n_ref[rows, col : col + size]
        at += size


def unpack(q_ref, got, swapped, count, p):
    half = p // 2
    core = lax.axis_index("gy") % 2
    width = q_ref.shape[1]
    at = 0
    for row, col, size in payload_blocks(count, p, width - q_ref.shape[0]):
        col = col % width
        for src, which in ((got, core), (swapped, 1 - core)):
            rows = pl.ds(pl.multiple_of(row + which * half, half), half)
            q_ref[rows, col : col + size] = src[:, at : at + size]
        at += size


def leaf_merge(own_map, own_flux, other_map, other_flux, n_ref, y_ref, send_ref, g):
    p = own_map.shape[0] // 4
    gx, gy = lax.axis_index("gx"), lax.axis_index("gy")
    lower = gy % 2 == 0
    low_group = (gy // 2) % 2 == 0
    f1 = pl.multiple_of(p * (1 - gx % 2), p)
    out = pl.multiple_of(p * (gx % 2), p)
    bottom, top = 2 * p, 3 * p

    def lo(r, c):
        at = (pl.ds(r, p), pl.ds(c, p))
        return jnp.where(lower, own_map[at], other_map[at])

    def up(r, c):
        at = (pl.ds(r, p), pl.ds(c, p))
        return jnp.where(lower, other_map[at], own_map[at])

    def lo_h(r):
        return jnp.where(lower, own_flux[pl.ds(r, p), :], other_flux[pl.ds(r, p), :])

    def up_h(r):
        return jnp.where(lower, other_flux[pl.ds(r, p), :], own_flux[pl.ds(r, p), :])

    g[:, 0:p] = lo(top, top) + up(bottom, bottom)
    g[:, p : 2 * p] = lo(top, f1)
    g[:, 2 * p : 3 * p] = up(bottom, f1)
    g[:, 3 * p : 4 * p] = jnp.where(low_group, up(bottom, top), lo(top, bottom))
    g[:, 4 * p : 5 * p] = lo(top, out)
    g[:, 5 * p : 6 * p] = up(bottom, out)
    g[:, 6 * p :] = lo_h(top) + up_h(bottom)
    none = jnp.zeros((p, p), F32)
    from_lo = jnp.where(low_group, 0.0, 1.0)
    from_up = 1.0 - from_lo
    blocks = [
        [lo(f1, f1), none, lo(f1, bottom) * from_lo, lo(f1, out), none, lo_h(f1)],
        [none, up(f1, f1), up(f1, top) * from_up, none, up(f1, out), up_h(f1)],
        [
            lo(bottom, f1) * from_lo,
            up(top, f1) * from_up,
            jnp.where(low_group, up(top, top), lo(bottom, bottom)),
            lo(bottom, out) * from_lo,
            up(top, out) * from_up,
            jnp.where(low_group, up_h(top), lo_h(bottom)),
        ],
        [lo(out, f1), none, lo(out, bottom) * from_lo, lo(out, out), none, lo_h(out)],
        [none, up(out, f1), up(out, top) * from_up, none, up(out, out), up_h(out)],
    ]
    for i, line in enumerate(blocks):
        for j, block in enumerate(line):
            n_ref[i * p : (i + 1) * p, j * p : j * p + block.shape[1]] = block
    block_solve(g, p, p, n_ref)
    y_ref[...] = g[:, p:]
    pack(send_ref, n_ref, 3, p)


def column_merge(n0, got, swapped, n_ref, y_ref, send_ref, g, q):
    p = n0.shape[0] // 5
    q[...] = jnp.zeros_like(q)
    unpack(q, got, swapped, 3, p)
    f, o, e = 2 * p, 3 * p, 5 * p
    g[:, 0:f] = n0[0:f, 0:f] + q[0:f, 0:f]
    g[:, f : f + p] = n0[0:f, f:o]
    g[:, f + p : f + 2 * p] = q[0:f, f:o]
    g[:, f + 2 * p : f + 4 * p] = n0[0:f, o:e]
    g[:, f + 4 * p :] = n0[0:f, e:] + q[0:f, o:]
    n_ref[...] = jnp.zeros_like(n_ref)
    n_ref[0:p, 0:p] = n0[f:o, f:o]
    n_ref[0:p, 2 * p :] = n0[f:o, o:]
    n_ref[p : 2 * p, p : 2 * p] = q[f:o, f:o]
    n_ref[p : 2 * p, 4 * p :] = q[f:o, o:]
    n_ref[2 * p :, 0:p] = n0[o:, f:o]
    n_ref[2 * p :, 2 * p :] = n0[o:, o:]
    block_solve(g, f, p, n_ref)
    y_ref[...] = g[:, f:]
    pack(send_ref, n_ref, 4, p)


def row_merge(n1, got, swapped, n_ref, y_ref, send_ref, g, q):
    p = n1.shape[0] // 4
    q[...] = jnp.zeros_like(q)
    unpack(q, got, swapped, 4, p)
    f = 2 * p
    g[:, 0:f] = n1[0:f, 0:f] + q[0:f, 0:f]
    g[:, f : 2 * f] = n1[0:f, f : 2 * f]
    g[:, 2 * f : 3 * f] = q[0:f, f : 2 * f]
    g[:, 3 * f :] = n1[0:f, 2 * f :] + q[0:f, 2 * f :]
    n_ref[...] = jnp.zeros_like(n_ref)
    n_ref[0:f, 0:f] = n1[f:, f : 2 * f]
    n_ref[0:f, 2 * f :] = n1[f:, 2 * f :]
    n_ref[f:, f:] = q[f:, f:]
    block_solve(g, f, p, n_ref)
    y_ref[...] = g[:, f:]
    pack(send_ref, n_ref, 4, p)


def top_solve(n2, got, swapped, y2, y1, u_ref, send_ref, g):
    p = n2.shape[0] // 4
    f = 2 * p
    g[...] = jnp.zeros_like(g)
    unpack(g, got, swapped, 4, p)
    g[...] += n2[...]
    block_solve(g, 4 * p, p)
    u3 = -g[:, 4 * p :]
    u2 = -(dot(y2[:, : 4 * p], u3) + y2[:, 4 * p :])
    u_ref[3 * p :, :] = u3[0:f]
    group = jnp.concatenate([u2, u3[0:f]], axis=0)
    u1 = -(dot(y1[:, : 4 * p], group) + y1[:, 4 * p :])
    u_ref[0:f, :] = u1
    u_ref[f : 3 * p, :] = u2[0:p]
    send_ref[0:f, :] = u1
    send_ref[f:, :] = u2[p:]


def leaf_values(own, got, y0, out_ref, u):
    p = own.shape[0] // 5
    gx, gy = lax.axis_index("gx"), lax.axis_index("gy")
    inner = (gx + 1) // 2 % 2 == 1
    lower = gy % 2 == 0
    low_group = (gy // 2) % 2 == 0
    u[0 : 3 * p, :] = jnp.where(inner, own[0 : 3 * p, :], got[...])
    u[3 * p :, :] = jnp.where(inner, own[3 * p :, :], 0.0)
    face = -(dot(y0[:, : 5 * p], u[...]) + y0[:, 5 * p :])
    spot = gy % 2
    near = u[pl.ds(pl.multiple_of(spot * p, p), p), :]
    far = u[pl.ds(pl.multiple_of((3 + spot) * p, p), p), :]
    cross = u[2 * p : 3 * p, :]
    f1_left = gx % 2 == 1
    out_ref[0:p, :] = jnp.where(f1_left, near, far)
    out_ref[p : 2 * p, :] = jnp.where(f1_left, far, near)
    out_ref[2 * p : 3 * p, :] = jnp.where(lower, jnp.where(low_group, 0.0, cross), face)
    out_ref[3 * p :, :] = jnp.where(lower, face, jnp.where(low_group, cross, 0.0))


def local(kernel, name, outs, scratch, *args):
    specs = [pl.BlockSpec(memory_space=pltpu.VMEM)]
    return pl.pallas_call(
        kernel,
        name=name,
        out_shape=[jax.ShapeDtypeStruct(shape, F32) for shape in outs],
        in_specs=specs * len(args),
        out_specs=specs * len(outs),
        scratch_shapes=[pltpu.VMEM(shape, F32) for shape in scratch],
        compiler_params=pltpu.CompilerParams(vmem_limit_bytes=48 << 20),
    )(*args)


def shards(leaf_maps, leaf_fluxes):
    p = leaf_maps.shape[2] // 4
    s = leaf_fluxes.shape[3]
    own_map, own_flux = leaf_maps[0, 0], leaf_fluxes[0, 0]
    columns, rows = lax.axis_size("gx"), lax.axis_size("gy")
    cores = [(i, i ^ 1) for i in range(rows)]
    groups = [(i, i ^ 2) for i in range(rows)]
    inner = [i for i in range(columns) if (i + 1) // 2 % 2 == 1]
    inward = [(i ^ 1, i) for i in inner]
    across = [(i, i ^ 3) for i in inner]
    outward = [(i, i ^ 1) for i in inner]

    def swap(x):
        return lax.ppermute(x, "gy", cores)

    other_map, other_flux = swap((own_map, own_flux))
    n0, y0, send = local(
        leaf_merge,
        "leaf_merge",
        [(5 * p, 5 * p + s), (p, 5 * p + s), (p // 2, 6 * p + 3 * s)],
        [(p, 6 * p + s)],
        own_map,
        own_flux,
        other_map,
        other_flux,
    )
    got = lax.ppermute(send, "gx", inward)
    n1, y1, send = local(
        column_merge,
        "column_merge",
        [(4 * p, 4 * p + s), (2 * p, 4 * p + s), (p // 2, 10 * p + 4 * s)],
        [(2 * p, 6 * p + s), (3 * p, 3 * p + s)],
        n0,
        got,
        swap(got),
    )
    got = lax.ppermute(send, "gy", groups)
    n2, y2, send = local(
        row_merge,
        "row_merge",
        [(4 * p, 4 * p + s), (2 * p, 4 * p + s), (p // 2, 10 * p + 4 * s)],
        [(2 * p, 6 * p + s), (4 * p, 4 * p + s)],
        n1,
        got,
        swap(got),
    )
    got = lax.ppermute(send, "gx", across)
    u, send = local(
        top_solve,
        "top_solve",
        [(5 * p, s), (3 * p, s)],
        [(4 * p, 4 * p + s)],
        n2,
        got,
        swap(got),
        y2,
        y1,
    )
    got = lax.ppermute(send, "gx", outward)
    (values,) = local(leaf_values, "leaf_values", [(4 * p, s)], [(5 * p, s)], u, got, y0)
    return values[None, None]


def solution(mesh):
    spec = P("gx", "gy", None, None)
    return jax.shard_map(
        shards, mesh=mesh, in_specs=(spec, spec), out_specs=spec, check_vma=False
    )
```

```python
import jax
import jax.numpy as jnp
from jax import lax
from jax.experimental import pallas as pl
from jax.experimental.pallas import tpu as pltpu
from jax.sharding import PartitionSpec as P

F32 = jnp.float32
HIGHEST = lax.Precision.HIGHEST
ROWS_DIM = (((0,), (0,)), ((), ()))
PANEL = 16


def dot(left, right):
    return jnp.dot(left, right, precision=HIGHEST, preferred_element_type=F32)


def tdot(left, right):
    return lax.dot_general(
        left, right, ROWS_DIM, precision=HIGHEST, preferred_element_type=F32
    )


def three_parts(x):
    first = x.astype(jnp.bfloat16)
    rest = x - first.astype(F32)
    second = rest.astype(jnp.bfloat16)
    third = (rest - second.astype(F32)).astype(jnp.bfloat16)
    return first, second, third


def tdot_thin(left, right):
    a, b, c = three_parts(left)
    d, e, f = three_parts(right)
    return lax.dot_general(
        jnp.concatenate([a, a, b, b, a, c], axis=0),
        jnp.concatenate([d, e, d, e, f, d], axis=0),
        ROWS_DIM,
        preferred_element_type=F32,
    )


def panel_solve(rows, rhs, first):
    width, lanes = rows.shape
    sub = lax.broadcasted_iota(jnp.int32, (width, lanes), 0)
    cols = [
        jnp.broadcast_to(rows[:, first + j : first + j + 1], (width, lanes))
        for j in range(width)
    ]
    for j in range(0, width, 2):
        c0, c1 = cols[j], cols[j + 1]
        aa, bb, dd = c0[j : j + 1], c1[j : j + 1], c1[j + 1 : j + 2]
        scale = 1.0 / (aa * dd - bb * bb)
        aa, bb, dd = aa * scale, bb * scale, dd * scale

        def step(x):
            x0, x1 = x[j : j + 1], x[j + 1 : j + 2]
            r0 = dd * x0 - bb * x1
            r1 = aa * x1 - bb * x0
            y = x - c0 * r0 - c1 * r1
            return jnp.where(sub == j, r0, jnp.where(sub == j + 1, r1, y))

        rhs = step(rhs)
        for m in range(j + 2, width):
            cols[m] = step(cols[m])
    return rhs


def spd_inverse(a):
    size = a.shape[0]
    row = lax.broadcasted_iota(jnp.int32, (PANEL, size), 0)
    col = lax.broadcasted_iota(jnp.int32, (PANEL, size), 1)
    for first in range(0, size, PANEL):
        rows = a[first : first + PANEL]
        v = rows - jnp.where(col == row + first, 1.0, 0.0)
        a = a - tdot_thin(v, panel_solve(rows, v, first))
    row = lax.broadcasted_iota(jnp.int32, (size, size), 0)
    col = lax.broadcasted_iota(jnp.int32, (size, size), 1)
    return jnp.where(row == col, 2.0, 0.0) - a


def block_solve(g, face, p, schur=None):
    pivot = g[0:p, 0:p]
    for k in range(0, face, p):
        head = g[k : k + p, k + p :]
        t = dot(spd_inverse(pivot), head)
        if k + p < face:
            after = slice(k + p, k + 2 * p)
            pivot = g[after, after] - tdot(head[:, :p], t[:, :p])
            g[k + p : face, k + p :] -= tdot(head[:, : face - k - p], t)
        if schur is not None:
            outer = head[:, face - k - p : face - k - p + schur.shape[0]]
            schur[...] -= tdot(outer, t[:, face - k - p :])
        g[k : k + p, k + p :] = t


def face_values(g, outer, p):
    face = g.shape[0]
    rest = g[:, face:] if outer is None else g[:, face + outer.shape[0] :]
    if outer is not None:
        rest = rest + dot(g[:, face : face + outer.shape[0]], outer)
    found = -rest[face - p :]
    for k in range(face - 2 * p, -1, -p):
        here = -rest[k : k + p] - dot(g[k : k + p, k + p : face], found)
        found = jnp.concatenate([here, found], axis=0)
    return found


def payload_blocks(count, p, s):
    spots = [(r * p, c * p, p) for r in range(count) for c in range(r, count)]
    return spots + [(r * p, -s, s) for r in range(count)]


def pack(send_ref, n_ref, count, p):
    half = p // 2
    core = lax.axis_index("gy") % 2
    width = n_ref.shape[1]
    at = 0
    for row, col, size in payload_blocks(count, p, width - n_ref.shape[0]):
        col = col % width
        rows = pl.ds(pl.multiple_of(row + core * half, half), half)
        send_ref[:, at : at + size] = n_ref[rows, col : col + size]
        at += size


def unpack(q_ref, got, swapped, count, p):
    half = p // 2
    core = lax.axis_index("gy") % 2
    width = q_ref.shape[1]
    at = 0
    for row, col, size in payload_blocks(count, p, width - q_ref.shape[0]):
        col = col % width
        for src, which in ((got, core), (swapped, 1 - core)):
            rows = pl.ds(pl.multiple_of(row + which * half, half), half)
            q_ref[rows, col : col + size] = src[:, at : at + size]
        at += size


def leaf_merge(own_map, own_flux, other_map, other_flux, n_ref, y_ref, send_ref, g):
    p = own_map.shape[0] // 4
    gx, gy = lax.axis_index("gx"), lax.axis_index("gy")
    lower = gy % 2 == 0
    low_group = (gy // 2) % 2 == 0
    f1 = pl.multiple_of(p * (1 - gx % 2), p)
    out = pl.multiple_of(p * (gx % 2), p)
    bottom, top = 2 * p, 3 * p

    def lo(r, c):
        at = (pl.ds(r, p), pl.ds(c, p))
        return jnp.where(lower, own_map[at], other_map[at])

    def up(r, c):
        at = (pl.ds(r, p), pl.ds(c, p))
        return jnp.where(lower, other_map[at], own_map[at])

    def lo_h(r):
        return jnp.where(lower, own_flux[pl.ds(r, p), :], other_flux[pl.ds(r, p), :])

    def up_h(r):
        return jnp.where(lower, other_flux[pl.ds(r, p), :], own_flux[pl.ds(r, p), :])

    g[:, 0:p] = lo(top, top) + up(bottom, bottom)
    g[:, p : 2 * p] = lo(top, f1)
    g[:, 2 * p : 3 * p] = up(bottom, f1)
    g[:, 3 * p : 4 * p] = jnp.where(low_group, up(bottom, top), lo(top, bottom))
    g[:, 4 * p : 5 * p] = lo(top, out)
    g[:, 5 * p : 6 * p] = up(bottom, out)
    g[:, 6 * p :] = lo_h(top) + up_h(bottom)
    none = jnp.zeros((p, p), F32)
    from_lo = jnp.where(low_group, 0.0, 1.0)
    from_up = 1.0 - from_lo
    blocks = [
        [lo(f1, f1), none, lo(f1, bottom) * from_lo, lo(f1, out), none, lo_h(f1)],
        [none, up(f1, f1), up(f1, top) * from_up, none, up(f1, out), up_h(f1)],
        [
            lo(bottom, f1) * from_lo,
            up(top, f1) * from_up,
            jnp.where(low_group, up(top, top), lo(bottom, bottom)),
            lo(bottom, out) * from_lo,
            up(top, out) * from_up,
            jnp.where(low_group, up_h(top), lo_h(bottom)),
        ],
        [lo(out, f1), none, lo(out, bottom) * from_lo, lo(out, out), none, lo_h(out)],
        [none, up(out, f1), up(out, top) * from_up, none, up(out, out), up_h(out)],
    ]
    for i, line in enumerate(blocks):
        for j, block in enumerate(line):
            n_ref[i * p : (i + 1) * p, j * p : j * p + block.shape[1]] = block
    block_solve(g, p, p, n_ref)
    y_ref[...] = g[:, p:]
    pack(send_ref, n_ref, 3, p)


def column_merge(n0, got, swapped, n_ref, g, send_ref, q):
    p = n0.shape[0] // 5
    q[...] = jnp.zeros_like(q)
    unpack(q, got, swapped, 3, p)
    f, o, e = 2 * p, 3 * p, 5 * p
    g[:, 0:f] = n0[0:f, 0:f] + q[0:f, 0:f]
    g[:, f : f + p] = n0[0:f, f:o]
    g[:, f + p : f + 2 * p] = q[0:f, f:o]
    g[:, f + 2 * p : f + 4 * p] = n0[0:f, o:e]
    g[:, f + 4 * p :] = n0[0:f, e:] + q[0:f, o:]
    n_ref[...] = jnp.zeros_like(n_ref)
    n_ref[0:p, 0:p] = n0[f:o, f:o]
    n_ref[0:p, 2 * p :] = n0[f:o, o:]
    n_ref[p : 2 * p, p : 2 * p] = q[f:o, f:o]
    n_ref[p : 2 * p, 4 * p :] = q[f:o, o:]
    n_ref[2 * p :, 0:p] = n0[o:, f:o]
    n_ref[2 * p :, 2 * p :] = n0[o:, o:]
    block_solve(g, f, p, n_ref)
    pack(send_ref, n_ref, 4, p)


def row_merge(n1, got, swapped, n_ref, g, send_ref, q):
    p = n1.shape[0] // 4
    q[...] = jnp.zeros_like(q)
    unpack(q, got, swapped, 4, p)
    f = 2 * p
    g[:, 0:f] = n1[0:f, 0:f] + q[0:f, 0:f]
    g[:, f : 2 * f] = n1[0:f, f : 2 * f]
    g[:, 2 * f : 3 * f] = q[0:f, f : 2 * f]
    g[:, 3 * f :] = n1[0:f, 2 * f :] + q[0:f, 2 * f :]
    n_ref[...] = jnp.zeros_like(n_ref)
    n_ref[0:f, 0:f] = n1[f:, f : 2 * f]
    n_ref[0:f, 2 * f :] = n1[f:, 2 * f :]
    n_ref[f:, f:] = q[f:, f:]
    block_solve(g, f, p, n_ref)
    pack(send_ref, n_ref, 4, p)


def top_solve(n2, got, swapped, y2, y1, u_ref, send_ref, g):
    p = n2.shape[0] // 4
    f = 2 * p
    g[...] = jnp.zeros_like(g)
    unpack(g, got, swapped, 4, p)
    g[...] += n2[...]
    block_solve(g, 4 * p, p)
    u3 = face_values(g, None, p)
    u2 = face_values(y2, u3, p)
    u_ref[3 * p :, :] = u3[0:f]
    group = jnp.concatenate([u2, u3[0:f]], axis=0)
    u1 = face_values(y1, group, p)
    u_ref[0:f, :] = u1
    u_ref[f : 3 * p, :] = u2[0:p]
    send_ref[0:f, :] = u1
    send_ref[f:, :] = u2[p:]


def leaf_values(own, got, y0, out_ref, u):
    p = own.shape[0] // 5
    gx, gy = lax.axis_index("gx"), lax.axis_index("gy")
    inner = (gx + 1) // 2 % 2 == 1
    lower = gy % 2 == 0
    low_group = (gy // 2) % 2 == 0
    u[0 : 3 * p, :] = jnp.where(inner, own[0 : 3 * p, :], got[...])
    u[3 * p :, :] = jnp.where(inner, own[3 * p :, :], 0.0)
    face = -(dot(y0[:, : 5 * p], u[...]) + y0[:, 5 * p :])
    spot = gy % 2
    near = u[pl.ds(pl.multiple_of(spot * p, p), p), :]
    far = u[pl.ds(pl.multiple_of((3 + spot) * p, p), p), :]
    cross = u[2 * p : 3 * p, :]
    f1_left = gx % 2 == 1
    out_ref[0:p, :] = jnp.where(f1_left, near, far)
    out_ref[p : 2 * p, :] = jnp.where(f1_left, far, near)
    out_ref[2 * p : 3 * p, :] = jnp.where(lower, jnp.where(low_group, 0.0, cross), face)
    out_ref[3 * p :, :] = jnp.where(lower, face, jnp.where(low_group, cross, 0.0))


def local(kernel, name, outs, scratch, *args):
    specs = [pl.BlockSpec(memory_space=pltpu.VMEM)]
    return pl.pallas_call(
        kernel,
        name=name,
        out_shape=[jax.ShapeDtypeStruct(shape, F32) for shape in outs],
        in_specs=specs * len(args),
        out_specs=specs * len(outs),
        scratch_shapes=[pltpu.VMEM(shape, F32) for shape in scratch],
        compiler_params=pltpu.CompilerParams(vmem_limit_bytes=48 << 20),
    )(*args)


def shards(leaf_maps, leaf_fluxes):
    p = leaf_maps.shape[2] // 4
    s = leaf_fluxes.shape[3]
    own_map, own_flux = leaf_maps[0, 0], leaf_fluxes[0, 0]
    columns, rows = lax.axis_size("gx"), lax.axis_size("gy")
    cores = [(i, i ^ 1) for i in range(rows)]
    groups = [(i, i ^ 2) for i in range(rows)]
    inner = [i for i in range(columns) if (i + 1) // 2 % 2 == 1]
    inward = [(i ^ 1, i) for i in inner]
    across = [(i, i ^ 3) for i in inner]
    outward = [(i, i ^ 1) for i in inner]

    def swap(x):
        return lax.ppermute(x, "gy", cores)

    other_map, other_flux = swap((own_map, own_flux))
    n0, y0, send = local(
        leaf_merge,
        "leaf_merge",
        [(5 * p, 5 * p + s), (p, 5 * p + s), (p // 2, 6 * p + 3 * s)],
        [(p, 6 * p + s)],
        own_map,
        own_flux,
        other_map,
        other_flux,
    )
    got = lax.ppermute(send, "gx", inward)
    n1, y1, send = local(
        column_merge,
        "column_merge",
        [(4 * p, 4 * p + s), (2 * p, 6 * p + s), (p // 2, 10 * p + 4 * s)],
        [(3 * p, 3 * p + s)],
        n0,
        got,
        swap(got),
    )
    got = lax.ppermute(send, "gy", groups)
    n2, y2, send = local(
        row_merge,
        "row_merge",
        [(4 * p, 4 * p + s), (2 * p, 6 * p + s), (p // 2, 10 * p + 4 * s)],
        [(4 * p, 4 * p + s)],
        n1,
        got,
        swap(got),
    )
    got = lax.ppermute(send, "gx", across)
    u, send = local(
        top_solve,
        "top_solve",
        [(5 * p, s), (3 * p, s)],
        [(4 * p, 4 * p + s)],
        n2,
        got,
        swap(got),
        y2,
        y1,
    )
    got = lax.ppermute(send, "gx", outward)
    (values,) = local(leaf_values, "leaf_values", [(4 * p, s)], [(5 * p, s)], u, got, y0)
    return values[None, None]


def solution(mesh):
    spec = P("gx", "gy", None, None)
    return jax.shard_map(
        shards, mesh=mesh, in_specs=(spec, spec), out_specs=spec, check_vma=False
    )
```
